1024 devices in a mesh: clu: 32 (over y, x, core), mem: 32 (over z).
Axes of the slice: x: 4, y: 4, z: 32, core: 2. Of those that a mesh axis runs over, the one named last changes fastest.
Arguments:
- seed_class: int32 [262144], P(('clu', 'mem')), may hold values from 0 to 15
- seed_weight: float32 [262144], P(('clu', 'mem')), may hold values from 0.3 to 3
- tile_values: bfloat16 [32, 32, 96, 128, 128], P('clu', 'mem'), may hold values from 0 to 1
- tile_rows: int32 [32, 32, 96], P('clu', 'mem'), may hold values from 0 to 63
- tile_cols: int32 [32, 32, 96], P('clu', 'mem'), may hold values from 0 to 63
- tile_count: int32 [32, 32], P('clu', 'mem'), may hold values from 12 to 96, as said below
Outputs:
- scores: float32 [8, 262144], P(None, ('clu', 'mem'))
- residual: float32 [8, 262144], P(None, ('clu', 'mem'))
The draws below stay inside these ranges and needn't reach their ends.
Inputs may be any that keep to these rules, and one draw needn't show every extreme that they name: `tile_count`: some device uses all 96 slots in every draw.
All inputs are finite; a program needn't handle non-finite values.
Results may differ from the reference program's by a relative error of at most 0.0027.
Values may be sent and summed in bfloat16 or wider, within the bound.
No kernel may reach another device: no remote copies, remote signals or barrier semaphores. Data moves between devices by JAX's collectives and lax.ppermute only.
A program may use at most 32 MiB of HBM per device.

```python
import math
import jax
import jax.numpy as jnp
from jax import lax

TILE = 128
CLASSES = 8
NB_DEV = 2
TCAP = 96
ITERS = 2
NODES = 262144
RB = 64
CB = 64
N_CLU = 32
N_MEM = 32


def draw_tile_count(key, part):
    key = jax.random.fold_in(key, 11)
    first, second = jax.random.split(key)
    total = N_CLU * N_MEM
    lowest = max(TCAP // 8, 1)
    counts = jax.random.randint(first, (total,), lowest, TCAP + 1)
    heavy = jax.random.randint(second, (), 0, total)
    counts = jnp.where(jnp.arange(total) == heavy, TCAP, counts)
    return counts.reshape(N_CLU, N_MEM).astype(jnp.int32)


def sparse_tiles(key, lowest):
    first, second = jax.random.split(key)
    shape = (N_CLU, N_MEM, TCAP, TILE, TILE)
    keep = min(0.9, 56.0 / (TCAP // NB_DEV * TILE))
    kept = jax.random.bernoulli(first, keep, shape).astype(jnp.float32)
    values = jax.random.uniform(second, shape, jnp.float32, lowest, 1.0)
    return (kept * values).astype(jnp.bfloat16)


def draw_tile_values(key, part):
    key = jax.random.fold_in(key, 23)
    return sparse_tiles(key, 0.1)


def touch_ends(result, own_key, smallest, top_value):
    extent = result.shape
    index_at = [jax.random.randint(jax.random.fold_in(own_key, axis), (), 0, extent[axis]) for axis in range(len(extent))]
    result = result.at[tuple(index_at)].set(smallest)
    longest = extent.index(max(extent))
    index_at[longest] = (index_at[longest] + 1) % extent[longest]
    return result.at[tuple(index_at)].set(top_value)


def level_of(rng, extent, cuts, least, largest):
    factor_of, own = 1.0, jax.random.fold_in(rng, 6)
    for dim, blocks in cuts:
        draws = jnp.exp(jax.random.uniform(jax.random.fold_in(own, dim), (blocks,), jnp.float32, least / len(cuts), largest / len(cuts)))
        factor_of = factor_of * jnp.repeat(draws, extent[dim] // blocks).reshape([-1 if axis == dim else 1 for axis in range(len(extent))])
    return factor_of


def setup_inputs(seed: int = 0) -> dict:
    key_list = jax.random.split(jax.random.key(seed), 7)
    seed_class = touch_ends(jax.random.randint(key_list[0], (NODES,), 0, 2 * CLASSES), jax.random.fold_in(key_list[0], 1), 0, (2 * CLASSES) - 1).astype(jnp.int32)
    seed_weight = jnp.clip(jnp.exp(math.log(3.0) - 2.3025851 * jax.random.uniform(key_list[1], (NODES,), jnp.float32) ** level_of(key_list[1], (NODES,), ((0, 1024),), -0.2, 0.2)), 0.3, 3.0)
    tile_values = draw_tile_values(jax.random.fold_in(key_list[6], 71), 0)
    tile_rows = touch_ends(jax.random.randint(key_list[3], (N_CLU, N_MEM, TCAP), 0, RB), jax.random.fold_in(key_list[3], 1), 0, RB - 1).astype(jnp.int32)
    tile_cols = touch_ends(jax.random.randint(key_list[4], (N_CLU, N_MEM, TCAP), 0, CB), jax.random.fold_in(key_list[4], 1), 0, CB - 1).astype(jnp.int32)
    tile_count = draw_tile_count(jax.random.fold_in(key_list[6], 71), 0)
    return dict(seed_class=seed_class, seed_weight=seed_weight, tile_values=tile_values, tile_rows=tile_rows, tile_cols=tile_cols, tile_count=tile_count)


def layout(tile_rows, tile_cols, tile_count):
    valid = (jnp.arange(TCAP, dtype=jnp.int32)[None, None, :] < tile_count[:, :, None]).astype(jnp.float32)
    global_rows = (jnp.arange(N_CLU, dtype=jnp.int32)[:, None, None] * RB + tile_rows).astype(jnp.int32)
    member = jnp.arange(N_MEM, dtype=jnp.int32)[None, :, None]
    global_cols = ((tile_cols // NB_DEV * N_MEM + member) * NB_DEV + tile_cols % NB_DEV).astype(jnp.int32)
    return (valid, global_rows, global_cols)

def reference(seed_class, seed_weight, tile_values, tile_rows, tile_cols, tile_count):
    blocks = NODES // TILE
    valid, global_rows, global_cols = layout(tile_rows, tile_cols, tile_count)

    def degree_step(carry, index):
        tiles_now = tile_values[index].astype(jnp.float32)
        mask = valid[index][:, :, None]
        row_part = lax.optimization_barrier(jnp.sum(tiles_now, axis=3)) * mask
        col_part = lax.optimization_barrier(jnp.sum(tiles_now, axis=2)) * mask
        carry = carry.at[global_rows[index]].add(row_part)
        carry = carry.at[global_cols[index]].add(col_part)
        return (carry, None)
    start = jnp.zeros((blocks, TILE), jnp.float32)
    summed, _ = lax.scan(degree_step, start, jnp.arange(N_CLU, dtype=jnp.int32))
    degree = 1.0 + summed.reshape(NODES)
    inverse_root = lax.rsqrt(degree)

    def operate(panel):
        scaled = lax.optimization_barrier((inverse_root[None, :] * panel).astype(jnp.bfloat16)).astype(jnp.float32)
        blocked = jnp.transpose(scaled.reshape(CLASSES, blocks, TILE), (1, 0, 2))

        def apply_step(carry, index):
            tiles_now = tile_values[index].astype(jnp.float32)
            mask = valid[index][:, :, None, None]
            from_cols = blocked[global_cols[index]]
            forward = jnp.einsum('mtij,mtcj->mtci', tiles_now, from_cols) * mask
            from_rows = blocked[global_rows[index]]
            backward = jnp.einsum('mtij,mtci->mtcj', tiles_now, from_rows) * mask
            carry = carry.at[global_rows[index]].add(forward)
            carry = carry.at[global_cols[index]].add(backward)
            return (carry, None)
        start_sum = jnp.zeros((blocks, CLASSES, TILE), jnp.float32)
        image_sum, _ = lax.scan(apply_step, start_sum, jnp.arange(N_CLU, dtype=jnp.int32))
        image_sum = jnp.transpose(image_sum, (1, 0, 2)).reshape(CLASSES, NODES)
        return panel - 0.99 * inverse_root[None, :] * image_sum
    classes_now = jnp.arange(CLASSES, dtype=jnp.int32)[:, None]
    labels = jnp.where(seed_class[None, :] == classes_now, seed_weight[None, :], jnp.float32(0.0)).astype(jnp.float32)
    scores = jnp.zeros_like(labels)
    residual = labels
    direction = labels
    norm_now = lax.optimization_barrier(jnp.sum(residual * residual, axis=1))
    for step in range(ITERS):
        image = operate(direction)
        alpha = norm_now / lax.optimization_barrier(jnp.sum(direction * image, axis=1))
        scores = scores + alpha[:, None] * direction
        residual = residual - alpha[:, None] * image
        if step + 1 < ITERS:
            norm_next = lax.optimization_barrier(jnp.sum(residual * residual, axis=1))
            direction = residual + (norm_next / norm_now)[:, None] * direction
            norm_now = norm_next
    return (scores, residual)
```

```python
import jax
import jax.numpy as jnp
from jax import lax
from jax.sharding import PartitionSpec as P

CLASSES = 8
NB_DEV = 2
DAMP = 0.99
F32 = jnp.float32
BF16 = jnp.bfloat16
HIGHEST = lax.Precision.HIGHEST


def swap(parts, axis):
    return lax.all_to_all(parts, axis, 0, 0, tiled=True)


def gather(own, axis):
    size = lax.axis_size(axis)
    return swap(jnp.broadcast_to(own[None], (size,) + own.shape), axis)


def split3(x):
    high = lax.reduce_precision(x, 8, 7)
    rest = x - high
    mid = lax.reduce_precision(rest, 8, 7)
    return jnp.concatenate([high, mid, rest - mid]).astype(BF16)


def on_device(seed_class, seed_weight, tile_values, tile_rows, tile_cols, tile_count):
    tiles = tile_values[0, 0]
    rows = tile_rows[0, 0]
    cols = tile_cols[0, 0]
    count = tile_count[0, 0]
    slots, side = tiles.shape[0], tiles.shape[1]
    n_mem, n_clu = lax.axis_size("mem"), lax.axis_size("clu")
    row_blocks, col_blocks = NB_DEV * n_mem, NB_DEV * n_clu
    valid = (jnp.arange(slots, dtype=jnp.int32) < count).astype(F32)
    row_table = (rows[None, :] == jnp.arange(row_blocks, dtype=jnp.int32)[:, None]).astype(F32) * valid
    col_table = (cols[None, :] == jnp.arange(col_blocks, dtype=jnp.int32)[:, None]).astype(F32) * valid

    row_totals = jnp.sum(tiles, axis=2, dtype=F32)
    col_totals = jnp.sum(tiles, axis=1, dtype=F32)
    row_part = jnp.einsum("rt,ti->ri", row_table, row_totals, precision=HIGHEST)
    col_part = jnp.einsum("kt,tj->kj", col_table, col_totals, precision=HIGHEST)
    from_cols = swap(col_part.reshape(n_clu, 1, NB_DEV * side), "clu")
    from_rows = swap(row_part.reshape(n_mem, 1, NB_DEV * side), "mem")
    degree = 1.0 + jnp.sum(from_cols, axis=0) + jnp.sum(from_rows, axis=0)
    inverse_root = lax.rsqrt(degree).reshape(NB_DEV, side)

    kinds = seed_class.reshape(NB_DEV, side)
    weight = seed_weight.reshape(NB_DEV, side)
    own = jnp.concatenate([(inverse_root * weight).astype(BF16), kinds.astype(BF16)])
    row_own = gather(own, "mem")
    col_own = gather(own, "clu")
    classes_now = jnp.arange(CLASSES, dtype=jnp.int32)[:, None]

    def panel_of(gathered):
        value = gathered[:, :NB_DEV].reshape(-1, 1, side)
        kind = gathered[:, NB_DEV:].reshape(-1, 1, side)
        return jnp.where(kind == classes_now.astype(BF16), value, jnp.zeros((), BF16))

    labels = jnp.where(kinds[:, None] == classes_now, weight[:, None], jnp.float32(0.0))
    scale = inverse_root[:, None]

    def products(row_panel, col_panel):
        forward = jnp.einsum(
            "tij,tcj->tci", tiles, jnp.take(col_panel, cols, axis=0), preferred_element_type=F32
        )
        backward = jnp.einsum(
            "tij,tci->tcj", tiles, jnp.take(row_panel, rows, axis=0), preferred_element_type=F32
        )
        row_sum = jnp.einsum("rt,tci->rci", row_table, forward, precision=HIGHEST)
        col_sum = jnp.einsum("kt,tcj->kcj", col_table, backward, precision=HIGHEST)
        return row_sum, col_sum

    height = NB_DEV * CLASSES
    row_sum, col_sum = products(panel_of(row_own), panel_of(col_own))
    from_cols = jnp.sum(swap(col_sum.reshape(n_clu, height, side), "clu"), axis=0)
    from_rows = jnp.sum(swap(row_sum.astype(BF16).reshape(n_mem, height, side), "mem").astype(F32), axis=0)
    first = scale * (from_cols + from_rows).reshape(NB_DEV, CLASSES, side)

    scaled = scale * first
    col_scaled = gather(scaled.reshape(height, side), "clu").reshape(col_blocks, CLASSES, side)
    row_scaled = gather(scaled.astype(BF16).reshape(height, side), "mem").reshape(row_blocks, CLASSES, side)
    row_sum, col_sum = products(row_scaled, col_scaled.astype(BF16))
    moments = jnp.concatenate(
        [
            jnp.sum(labels * labels, axis=(0, 2)),
            jnp.sum(labels * first, axis=(0, 2)),
            jnp.sum(first * first, axis=(0, 2)),
            2.0 * jnp.sum(col_scaled * col_sum, axis=(0, 2)),
        ]
    )
    pieces = split3(moments)
    extra = jnp.zeros((8, side), BF16).at[0, : pieces.shape[0]].set(pieces)
    sent = jnp.concatenate(
        [
            row_sum.astype(BF16).reshape(n_mem, height, side),
            jnp.broadcast_to(extra[None], (n_mem, 8, side)),
        ],
        axis=1,
    )
    got = jnp.sum(swap(sent, "mem").astype(F32), axis=0)
    from_rows = got[:height]
    line = got[height:]
    sent = jnp.concatenate(
        [col_sum.reshape(n_clu, height, side), jnp.broadcast_to(line[None], (n_clu, 8, side))], axis=1
    )
    got = jnp.sum(swap(sent, "clu"), axis=0)
    second = scale * (got[:height] + from_rows).reshape(NB_DEV, CLASSES, side)
    m = got[height, : pieces.shape[0]].reshape(3, 4, CLASSES)
    m0, m1, m2, m3 = (m[0] + m[1] + m[2])[:, :, None]

    ratio = m1 / m0
    qq = m2 - ratio * m1
    q_image = m3 - ratio * (2.0 * qq + ratio * m1)
    alpha0 = m0 / (m0 - DAMP * m1)
    pace = DAMP * alpha0
    beta = pace * pace * qq / m0
    alpha1 = qq / (qq - DAMP * q_image - DAMP * pace * qq * (qq / m0))
    q = first - ratio * labels
    q_applied = q - DAMP * (second - ratio * first)
    direction = pace * q + beta * labels
    applied = pace * q_applied + beta * (labels - DAMP * first)
    scores = alpha0 * labels + alpha1 * direction
    residual = pace * q - alpha1 * applied

    def out(x):
        return jnp.swapaxes(x, 0, 1).reshape(CLASSES, NB_DEV * side)

    return (out(scores), out(residual))


def solution(mesh):
    in_specs = (
        P(("clu", "mem")),
        P(("clu", "mem")),
        P("clu", "mem", None, None, None),
        P("clu", "mem", None),
        P("clu", "mem", None),
        P("clu", "mem"),
    )
    out_specs = (P(None, ("clu", "mem")), P(None, ("clu", "mem")))
    return jax.shard_map(
        on_device, mesh=mesh, in_specs=in_specs, out_specs=out_specs, check_vma=False
    )
```

```python
import functools

import jax
import jax.numpy as jnp
from jax import lax
from jax.experimental import pallas as pl
from jax.experimental.pallas import tpu as pltpu
from jax.sharding import PartitionSpec as P

CLASSES = 8
NB_DEV = 2
DAMP = 0.99
F32 = jnp.float32
BF16 = jnp.bfloat16
STEP = 16
LIMIT = 8


def swap(parts, axis):
    return lax.all_to_all(parts, axis, 0, 0, tiled=True)


def gather_both(sent):
    n_mem, n_clu = lax.axis_size("mem"), lax.axis_size("clu")
    from_clu = swap(sent[:n_clu], "clu")
    sent, from_clu = lax.optimization_barrier((sent, from_clu))
    return from_clu, swap(sent[:n_mem], "mem")


def split3(x):
    high = lax.reduce_precision(x, 8, 7)
    rest = x - high
    mid = lax.reduce_precision(rest, 8, 7)
    return jnp.concatenate([high, mid, rest - mid]).astype(BF16)


def sum_slots(slots_ref, count_ref, tiles_ref, acc, left_of, side):
    step = pl.program_id(0)
    into = slots_ref

    @pl.when(step == 0)
    def _():
        acc[...] = jnp.zeros_like(acc)

    for t in range(STEP):
        slot = step * STEP + t
        block = into[slot]
        used = jnp.where(slot < count_ref[0], 1.0, 0.0)
        product = lax.dot_general(
            left_of(slot), tiles_ref[t], (((1,), (side,)), ((), ())), preferred_element_type=F32
        )
        acc[block] += used * product


def totals_kernel(side, into_ref, count_ref, tiles_ref, out, acc):
    ones = jnp.ones((CLASSES, tiles_ref.shape[2]), BF16)
    sum_slots(into_ref, count_ref, tiles_ref, acc, lambda slot: ones, side)

    @pl.when(pl.program_id(0) == pl.num_programs(0) - 1)
    def _():
        out[...] = acc[:, 0, :]


def products_kernel(side, into_ref, count_ref, from_ref, panel, tiles_ref, out, acc, wide):
    @pl.when(pl.program_id(0) == 0)
    def _():
        wide[...] = panel[...].astype(F32).reshape(wide.shape)

    sum_slots(
        into_ref, count_ref, tiles_ref, acc, lambda slot: wide[from_ref[slot]].astype(BF16), side
    )

    @pl.when(pl.program_id(0) == pl.num_programs(0) - 1)
    def _():
        out[...] = acc[...].reshape(out.shape).astype(out.dtype)


def middle_kernel(from_cols, from_rows, scale, first, sent):
    scale = scale[...]
    image = jnp.sum(from_cols[...].astype(F32), axis=0) + jnp.sum(from_rows[...].astype(F32), axis=0)
    image = scale * image
    first[...] = image
    sent[...] = jnp.broadcast_to((scale * image).astype(BF16)[None], sent.shape)


def call_on_tiles(kernel, index, panels, tiles, out, scratch, limit):
    slots, side = tiles.shape[0], tiles.shape[1]

    def whole(x):
        return pl.BlockSpec(x.shape, lambda i, *_: (0,) * len(x.shape))

    return pl.pallas_call(
        kernel,
        grid_spec=pltpu.PrefetchScalarGridSpec(
            num_scalar_prefetch=len(index),
            grid=(slots // STEP,),
            in_specs=[whole(p) for p in panels]
            + [pl.BlockSpec((STEP, side, side), lambda i, *_: (i, 0, 0))],
            out_specs=whole(out),
            scratch_shapes=[pltpu.VMEM(x, F32) for x in scratch],
        ),
        out_shape=out,
        compiler_params=pltpu.CompilerParams(
            dimension_semantics=("arbitrary",), vmem_limit_bytes=limit << 20
        ),
        cost_estimate=pl.CostEstimate(
            flops=2 * CLASSES * slots * side * side,
            bytes_accessed=2 * slots * side * side,
            transcendentals=0,
        ),
    )(*index, *panels, tiles)


def on_device(seed_class, seed_weight, tile_values, tile_rows, tile_cols, tile_count):
    tiles = tile_values[0, 0]
    rows = tile_rows[0, 0]
    cols = tile_cols[0, 0]
    count = tile_count[0]
    slots, side = tiles.shape[0], tiles.shape[1]
    n_mem, n_clu = lax.axis_size("mem"), lax.axis_size("clu")
    row_blocks, col_blocks = NB_DEV * n_mem, NB_DEV * n_clu
    height = NB_DEV * CLASSES
    row_space, col_space = (row_blocks, CLASSES, side), (col_blocks, CLASSES, side)
    shape = jax.ShapeDtypeStruct

    used = jnp.arange(slots, dtype=jnp.int32) < count
    blocks = jnp.arange(col_blocks, dtype=jnp.int32)[:, None]
    col_table = ((cols[None, :] == blocks) & used).astype(F32)
    col_totals = jnp.sum(tiles, axis=1, dtype=F32)
    col_part = jnp.einsum("kt,tj->kj", col_table, col_totals, precision=lax.Precision.HIGHEST)
    row_part = call_on_tiles(
        functools.partial(totals_kernel, 1), (rows, count), (), tiles,
        shape((row_blocks, side), F32), (row_space,), LIMIT,
    )
    from_cols = swap(col_part.reshape(n_clu, NB_DEV, side), "clu")
    row_part, from_cols = lax.optimization_barrier((row_part, from_cols))
    from_rows = swap(row_part.reshape(n_mem, NB_DEV, side), "mem")
    degree = 1.0 + jnp.sum(from_cols, axis=0) + jnp.sum(from_rows, axis=0)
    inverse_root = lax.rsqrt(degree)

    kinds = seed_class.reshape(NB_DEV, side)
    weight = seed_weight.reshape(NB_DEV, side)
    own = jnp.concatenate([(inverse_root * weight).astype(BF16), kinds.astype(BF16)])
    peers = max(n_mem, n_clu)
    col_own, row_own = gather_both(jnp.broadcast_to(own[None], (peers,) + own.shape))
    kinds, weight, row_own = lax.optimization_barrier((kinds, weight, row_own))
    classes_now = jnp.arange(CLASSES, dtype=jnp.int32)[:, None]

    def panel_of(gathered):
        value = gathered[:, :NB_DEV].reshape(-1, 1, side)
        kind = gathered[:, NB_DEV:].reshape(-1, 1, side)
        return jnp.where(kind == classes_now.astype(BF16), value, jnp.zeros((), BF16))

    labels = jnp.where(kinds[:, None] == classes_now, weight[:, None], jnp.float32(0.0))
    scale = inverse_root[:, None]

    def forward(col_panel):
        return call_on_tiles(
            functools.partial(products_kernel, 1), (rows, count, cols), (col_panel,), tiles,
            shape((n_mem, height, side), BF16), (row_space, col_space), LIMIT,
        )

    def backward(row_panel, dtype):
        return call_on_tiles(
            functools.partial(products_kernel, 0), (cols, count, rows), (row_panel,), tiles,
            shape((n_clu, height, side), dtype), (col_space, row_space), LIMIT,
        )

    def total(parts):
        return jnp.sum(parts.astype(F32), axis=0)

    row_sum = forward(panel_of(col_own).reshape(n_clu, height, side))
    row_sum, row_own = lax.optimization_barrier((row_sum, row_own))
    from_rows = swap(row_sum, "mem")
    col_sum = backward(panel_of(row_own).reshape(n_mem, height, side), F32)
    col_sum, from_rows = lax.optimization_barrier((col_sum, from_rows))
    from_cols = swap(col_sum, "clu")
    first, sent = pl.pallas_call(
        middle_kernel,
        out_shape=(shape((height, side), F32), shape((peers, height, side), BF16)),
        compiler_params=pltpu.CompilerParams(vmem_limit_bytes=LIMIT << 20),
    )(from_cols, from_rows, jnp.broadcast_to(scale, (NB_DEV, CLASSES, side)).reshape(height, side))
    first = first.reshape(NB_DEV, CLASSES, side)

    col_scaled, row_scaled = gather_both(sent)

    def wide(partials):
        return jnp.pad(partials.reshape(-1, NB_DEV, CLASSES * side), ((0, 0), (0, 0), (0, side)))

    row_sum = forward(col_scaled)
    row_wide = wide(row_sum)
    row_sum, row_wide, row_scaled = lax.optimization_barrier((row_sum, row_wide, row_scaled))
    dots = total(row_sum.astype(F32) * row_scaled.astype(F32)).reshape(NB_DEV, CLASSES, side)
    moments = jnp.concatenate(
        [
            jnp.sum(labels * labels, axis=(0, 2)),
            jnp.sum(labels * first, axis=(0, 2)),
            jnp.sum(first * first, axis=(0, 2)),
            2.0 * jnp.sum(dots, axis=(0, 2)),
        ]
    )
    def with_moments(partials, moments):
        pieces = split3(moments)
        pieces = jnp.pad(pieces[None], ((0, NB_DEV - 1), (0, side - pieces.shape[0])))
        pieces = jnp.broadcast_to(pieces[None], (partials.shape[0],) + pieces.shape)
        return lax.dynamic_update_slice(partials, pieces, (0, 0, CLASSES * side))

    def moments_of(swapped):
        pieces = jnp.sum(swapped[:, 0, CLASSES * side :].astype(F32), axis=0)
        return jnp.sum(pieces[: 3 * 4 * CLASSES].reshape(3, -1), axis=0)

    from_rows = swap(with_moments(row_wide, moments), "mem")
    col_wide = wide(backward(row_scaled, BF16))
    col_wide, from_rows = lax.optimization_barrier((col_wide, from_rows))
    from_cols = swap(with_moments(col_wide, moments_of(from_rows)), "clu")
    image = total(from_cols) + total(from_rows)
    second = scale * image[:, : CLASSES * side].reshape(NB_DEV, CLASSES, side)
    m0, m1, m2, m3 = moments_of(from_cols).reshape(4, CLASSES)[:, :, None]

    ratio = m1 / m0
    qq = m2 - ratio * m1
    q_image = m3 - ratio * (2.0 * qq + ratio * m1)
    alpha0 = m0 / (m0 - DAMP * m1)
    pace = DAMP * alpha0
    beta = pace * pace * qq / m0
    alpha1 = qq / (qq - DAMP * q_image - DAMP * pace * qq * (qq / m0))
    q = first - ratio * labels
    q_applied = q - DAMP * (second - ratio * first)
    direction = pace * q + beta * labels
    applied = pace * q_applied + beta * (labels - DAMP * first)
    scores = alpha0 * labels + alpha1 * direction
    residual = pace * q - alpha1 * applied

    def out(x):
        return jnp.swapaxes(x, 0, 1).reshape(CLASSES, NB_DEV * side)

    return (out(scores), out(residual))


def solution(mesh):
    in_specs = (
        P(("clu", "mem")),
        P(("clu", "mem")),
        P("clu", "mem", None, None, None),
        P("clu", "mem", None),
        P("clu", "mem", None),
        P("clu", "mem"),
    )
    out_specs = (P(None, ("clu", "mem")), P(None, ("clu", "mem")))
    return jax.shard_map(
        on_device, mesh=mesh, in_specs=in_specs, out_specs=out_specs, check_vma=False
    )
```

```python
import functools

import jax
import jax.numpy as jnp
from jax import lax
from jax.experimental import pallas as pl
from jax.experimental.pallas import tpu as pltpu
from jax.sharding import PartitionSpec as P

CLASSES = 8
NB_DEV = 2
DAMP = 0.99
F32 = jnp.float32
BF16 = jnp.bfloat16
STEP = 32
LIMIT = 8


def swap(parts, axis):
    return lax.all_to_all(parts, axis, 0, 0, tiled=True)


def split3(x):
    high = lax.reduce_precision(x, 8, 7)
    rest = x - high
    mid = lax.reduce_precision(rest, 8, 7)
    return jnp.concatenate([high, mid, rest - mid]).astype(BF16)


def sum_slots(into_ref, count_ref, tiles_ref, acc, left_of, side):
    acc[...] = jnp.zeros_like(acc)
    for slot in range(tiles_ref.shape[0]):
        used = jnp.where(slot < count_ref[0], 1.0, 0.0)
        product = lax.dot_general(
            left_of(slot), tiles_ref[slot], (((1,), (side,)), ((), ())), preferred_element_type=F32
        )
        acc[into_ref[slot]] += used * product


def totals_kernel(side, into_ref, count_ref, tiles_ref, out, acc):
    ones = jnp.ones((CLASSES, tiles_ref.shape[2]), BF16)
    sum_slots(into_ref, count_ref, tiles_ref, acc, lambda slot: ones, side)
    out[...] = acc[:, 0, :]


def products_kernel(side, into_ref, count_ref, from_ref, panel, tiles_ref, out, acc, wide):
    wide[...] = panel[...].astype(F32).reshape(wide.shape)
    sum_slots(
        into_ref, count_ref, tiles_ref, acc, lambda slot: wide[from_ref[slot]].astype(BF16), side
    )
    out[...] = acc[...].reshape(out.shape).astype(out.dtype)


def middle_kernel(from_cols, row_image, scale, first, sent):
    scale = scale[...]
    image = scale * (jnp.sum(from_cols[...], axis=0) + row_image[...])
    first[...] = image
    sent[...] = jnp.broadcast_to((scale * image).astype(BF16)[None], sent.shape)


def call_on_tiles(kernel, index, panels, tiles, out, scratch, limit):
    slots, side = tiles.shape[0], tiles.shape[1]

    smem, vmem = pl.BlockSpec(memory_space=pltpu.SMEM), pl.BlockSpec(memory_space=pltpu.VMEM)
    return pl.pallas_call(
        kernel,
        in_specs=[smem] * len(index) + [vmem] * (len(panels) + 1),
        out_specs=vmem,
        scratch_shapes=[pltpu.VMEM(x, F32) for x in scratch],
        out_shape=out,
        compiler_params=pltpu.CompilerParams(vmem_limit_bytes=limit << 20),
        cost_estimate=pl.CostEstimate(
            flops=2 * CLASSES * slots * side * side,
            bytes_accessed=2 * slots * side * side,
            transcendentals=0,
        ),
    )(*index, *panels, tiles)


def on_device(seed_class, seed_weight, tile_values, tile_rows, tile_cols, tile_count):
    tiles = tile_values[0, 0]
    rows = tile_rows[0, 0]
    cols = tile_cols[0, 0]
    count = tile_count[0]
    slots, side = tiles.shape[0], tiles.shape[1]
    n_mem, n_clu = lax.axis_size("mem"), lax.axis_size("clu")
    row_blocks, col_blocks = NB_DEV * n_mem, NB_DEV * n_clu
    height = NB_DEV * CLASSES
    row_space, col_space = (row_blocks, CLASSES, side), (col_blocks, CLASSES, side)
    shape = jax.ShapeDtypeStruct

    used = jnp.arange(slots, dtype=jnp.int32) < count
    blocks = jnp.arange(col_blocks, dtype=jnp.int32)[:, None]
    col_table = ((cols[None, :] == blocks) & used).astype(F32)
    col_totals = jnp.sum(tiles, axis=1, dtype=F32)
    col_part = jnp.einsum("kt,tj->kj", col_table, col_totals, precision=lax.Precision.HIGHEST)
    row_part = call_on_tiles(
        functools.partial(totals_kernel, 1), (rows, count), (), tiles,
        shape((row_blocks, side), F32), (row_space,), LIMIT,
    )
    from_cols = swap(col_part.reshape(n_clu, NB_DEV, side), "clu")
    row_part, from_cols = lax.optimization_barrier((row_part, from_cols))
    from_rows = swap(row_part.reshape(n_mem, NB_DEV, side), "mem")
    degree = 1.0 + jnp.sum(from_cols, axis=0) + jnp.sum(from_rows, axis=0)
    inverse_root = lax.rsqrt(degree)

    kinds = seed_class.reshape(NB_DEV, side)
    weight = seed_weight.reshape(NB_DEV, side)
    own = jnp.concatenate([inverse_root * weight, kinds.astype(F32)])
    peers = max(n_mem, n_clu)
    col_own = swap(jnp.broadcast_to(own.astype(BF16)[None], (n_clu,) + own.shape), "clu")
    classes_now = jnp.arange(CLASSES, dtype=jnp.int32)[:, None]

    def panel_of(value, kind):
        kind = kind.reshape(-1, 1, side)
        panel = jnp.where(kind == classes_now.astype(BF16), value.reshape(-1, 1, side), jnp.zeros((), BF16))
        return panel.reshape(-1, height, side)

    labels = jnp.where(kinds[:, None] == classes_now, weight[:, None], jnp.float32(0.0))
    scale = inverse_root[:, None]

    def forward(col_panel):
        return call_on_tiles(
            functools.partial(products_kernel, 1), (rows, count, cols), (col_panel,), tiles,
            shape((n_mem, height, side), BF16), (row_space, col_space), LIMIT,
        )

    def backward(row_panel, dtype):
        return call_on_tiles(
            functools.partial(products_kernel, 0), (cols, count, rows), (row_panel,), tiles,
            shape((n_clu, height, side), dtype), (col_space, row_space), LIMIT,
        )

    def total(parts):
        return jnp.sum(parts.astype(F32), axis=0)

    lanes = CLASSES * side

    def wide(partials, tail):
        partials = partials.reshape(-1, NB_DEV, lanes)
        tail = jnp.broadcast_to(tail[None].astype(BF16), partials.shape[:1] + tail.shape)
        return jnp.concatenate([partials, tail], axis=2)

    def narrow(image):
        return image[:, :lanes].reshape(NB_DEV, CLASSES, side)

    row_sum = forward(panel_of(col_own[:, :NB_DEV], col_own[:, NB_DEV:]))
    from_mem = swap(wide(row_sum, jnp.concatenate([own[:NB_DEV], own[NB_DEV:]], axis=1)), "mem")
    col_sum = backward(
        panel_of(from_mem[:, :, lanes : lanes + side], from_mem[:, :, lanes + side :]), F32
    )
    from_cols = swap(col_sum, "clu")
    row_image = narrow(total(from_mem)).reshape(height, side)
    first, sent = pl.pallas_call(
        middle_kernel,
        out_shape=(shape((height, side), F32), shape((peers, height, side), BF16)),
        compiler_params=pltpu.CompilerParams(vmem_limit_bytes=LIMIT << 20),
    )(from_cols, row_image, jnp.broadcast_to(scale, (NB_DEV, CLASSES, side)).reshape(height, side))
    first = first.reshape(NB_DEV, CLASSES, side)

    col_scaled = swap(sent[:n_clu], "clu")
    sent, col_scaled = lax.optimization_barrier((sent, col_scaled))
    row_scaled = swap(sent[:n_mem], "mem")
    def pieces_row(x):
        pieces = split3(x)
        return jnp.pad(pieces, (0, side - pieces.shape[0]))

    def whole(pieces, count):
        return jnp.sum(pieces[: 3 * count].reshape(3, count), axis=0)

    early = jnp.concatenate(
        [
            jnp.sum(labels * labels, axis=(0, 2)),
            jnp.sum(labels * first, axis=(0, 2)),
            jnp.sum(first * first, axis=(0, 2)),
        ]
    )
    row_sum = forward(col_scaled)
    row_wide = wide(row_sum, jnp.pad(pieces_row(early)[None], ((0, NB_DEV - 1), (0, 0))))
    row_sum, row_wide, row_scaled = lax.optimization_barrier((row_sum, row_wide, row_scaled))
    dots = 2.0 * jnp.sum(
        (row_sum.astype(F32) * row_scaled.astype(F32)).reshape(-1, NB_DEV, CLASSES, side), axis=(0, 1, 3)
    )
    is_late = jnp.arange(NB_DEV)[:, None] == 1
    spare = jnp.where(is_late, pieces_row(dots), row_wide[:, :, lanes:])
    from_rows = swap(lax.dynamic_update_slice(row_wide, spare, (0, 0, lanes)), "mem")
    col_sum = backward(row_scaled, BF16)
    col_sum, from_rows = lax.optimization_barrier((col_sum, from_rows))
    from_rows = lax.optimization_barrier(total(from_rows))
    line = from_rows[:, lanes:]
    line = pieces_row(jnp.concatenate([whole(line[0], 3 * CLASSES), whole(line[1], CLASSES)]))
    line = jnp.broadcast_to(jnp.pad(line[None], ((0, CLASSES - 1), (0, 0))), (n_clu, CLASSES, side))
    from_cols = swap(jnp.concatenate([col_sum, line], axis=1), "clu")
    from_cols, row_image = lax.optimization_barrier((from_cols, narrow(from_rows)))
    from_cols = total(from_cols)
    image = from_cols[:height].reshape(NB_DEV, CLASSES, side) + row_image
    second = scale * image
    m0, m1, m2, m3 = whole(from_cols[height], 4 * CLASSES).reshape(4, CLASSES)[:, :, None]

    ratio = m1 / m0
    qq = m2 - ratio * m1
    q_image = m3 - ratio * (2.0 * qq + ratio * m1)
    alpha0 = m0 / (m0 - DAMP * m1)
    pace = DAMP * alpha0
    beta = pace * pace * qq / m0
    alpha1 = qq / (qq - DAMP * q_image - DAMP * pace * qq * (qq / m0))
    q = first - ratio * labels
    q_applied = q - DAMP * (second - ratio * first)
    direction = pace * q + beta * labels
    applied = pace * q_applied + beta * (labels - DAMP * first)
    scores = alpha0 * labels + alpha1 * direction
    residual = pace * q - alpha1 * applied

    def out(x):
        return jnp.swapaxes(x, 0, 1).reshape(CLASSES, NB_DEV * side)

    return (out(scores), out(residual))


def solution(mesh):
    in_specs = (
        P(("clu", "mem")),
        P(("clu", "mem")),
        P("clu", "mem", None, None, None),
        P("clu", "mem", None),
        P("clu", "mem", None),
        P("clu", "mem"),
    )
    out_specs = (P(None, ("clu", "mem")), P(None, ("clu", "mem")))
    return jax.shard_map(
        on_device, mesh=mesh, in_specs=in_specs, out_specs=out_specs, check_vma=False
    )
```

```python
import functools

import jax
import jax.numpy as jnp
from jax import lax
from jax.experimental import pallas as pl
from jax.experimental.pallas import tpu as pltpu
from jax.sharding import PartitionSpec as P

CLASSES = 8
NB_DEV = 2
DAMP = 0.99
F32 = jnp.float32
BF16 = jnp.bfloat16
STEP = 32
LIMIT = 8
KIND_AT = 3 * NB_DEV
SUMS_AT = KIND_AT + NB_DEV


def swap(parts, axis):
    return lax.all_to_all(parts, axis, 0, 0, tiled=True)


def split3(x):
    high = lax.reduce_precision(x, 8, 7)
    rest = x - high
    mid = lax.reduce_precision(rest, 8, 7)
    return jnp.concatenate([high, mid, rest - mid]).astype(BF16)


def sum_slots(into_ref, count_ref, tiles_ref, acc, left_of, side):
    acc[...] = jnp.zeros_like(acc)
    for slot in range(tiles_ref.shape[0]):
        used = jnp.where(slot < count_ref[0], 1.0, 0.0)
        product = lax.dot_general(
            left_of(slot), tiles_ref[slot], (((1,), (side,)), ((), ())), preferred_element_type=F32
        )
        acc[into_ref[slot]] += used * product


def totals_kernel(side, into_ref, count_ref, tiles_ref, out, acc):
    ones = jnp.ones((CLASSES, tiles_ref.shape[2]), BF16)
    sum_slots(into_ref, count_ref, tiles_ref, acc, lambda slot: ones, side)
    out[...] = acc[:, 0, :]


def products_kernel(side, into_ref, count_ref, from_ref, panel, tiles_ref, out, acc, wide):
    wide[...] = panel[...].astype(F32).reshape(wide.shape)
    sum_slots(
        into_ref, count_ref, tiles_ref, acc, lambda slot: wide[from_ref[slot]].astype(BF16), side
    )
    out[...] = acc[...].reshape(out.shape).astype(out.dtype)


def first_kernel(into_ref, count_ref, from_ref, got, tiles_ref, out, root, acc, wide, known, value):
    n_clu = got.shape[0]
    blocks = NB_DEV * n_clu
    known[...] = got[:, blocks:].astype(F32)
    totals = jnp.sum(got[:, :blocks].astype(F32), axis=0)

    def whole(row):
        return known[:, row, :] + known[:, row + NB_DEV, :] + known[:, row + 2 * NB_DEV, :]

    for b in range(NB_DEV):
        part = slice(b * n_clu, (b + 1) * n_clu)
        root[part] = lax.rsqrt(1.0 + totals[part] + whole(SUMS_AT + b))
        value[part] = root[part] * whole(b)
    for b in range(NB_DEV):
        for peer in range(n_clu):
            block = b * n_clu + peer
            row = (CLASSES, value.shape[1])
            kind = jnp.broadcast_to(known[peer, KIND_AT + b : KIND_AT + b + 1, :], row)
            here = jnp.broadcast_to(value[block : block + 1, :], row)
            classes_now = lax.broadcasted_iota(jnp.int32, row, 0).astype(F32)
            wide[block] = jnp.where(kind == classes_now, here, 0.0)
    sum_slots(
        into_ref, count_ref, tiles_ref, acc, lambda slot: wide[from_ref[slot]].astype(BF16), 1
    )
    out[...] = acc[...].reshape(out.shape).astype(out.dtype)


def middle_kernel(from_cols, row_image, scale, first, sent):
    scale = scale[...]
    image = scale * (jnp.sum(from_cols[...], axis=0) + row_image[...])
    first[...] = image
    sent[...] = jnp.broadcast_to((scale * image).astype(BF16)[None], sent.shape)


def call_on_tiles(kernel, index, panels, tiles, out, scratch, limit):
    slots, side = tiles.shape[0], tiles.shape[1]

    smem, vmem = pl.BlockSpec(memory_space=pltpu.SMEM), pl.BlockSpec(memory_space=pltpu.VMEM)
    return pl.pallas_call(
        kernel,
        in_specs=[smem] * len(index) + [vmem] * (len(panels) + 1),
        out_specs=jax.tree.map(lambda _: vmem, out),
        scratch_shapes=[pltpu.VMEM(x, F32) for x in scratch],
        out_shape=out,
        compiler_params=pltpu.CompilerParams(vmem_limit_bytes=limit << 20),
        cost_estimate=pl.CostEstimate(
            flops=2 * CLASSES * slots * side * side,
            bytes_accessed=2 * slots * side * side,
            transcendentals=0,
        ),
    )(*index, *panels, tiles)


def on_device(seed_class, seed_weight, tile_values, tile_rows, tile_cols, tile_count):
    tiles = tile_values[0, 0]
    rows = tile_rows[0, 0]
    cols = tile_cols[0, 0]
    count = tile_count[0]
    slots, side = tiles.shape[0], tiles.shape[1]
    n_mem, n_clu = lax.axis_size("mem"), lax.axis_size("clu")
    row_blocks, col_blocks = NB_DEV * n_mem, NB_DEV * n_clu
    height = NB_DEV * CLASSES
    row_space, col_space = (row_blocks, CLASSES, side), (col_blocks, CLASSES, side)
    shape = jax.ShapeDtypeStruct

    used = jnp.arange(slots, dtype=jnp.int32) < count
    blocks = jnp.arange(row_blocks, dtype=jnp.int32)[:, None]
    row_table = ((rows[None, :] == blocks) & used).astype(F32)
    row_totals = jnp.sum(tiles, axis=2, dtype=F32)
    row_part = jnp.einsum("rt,ti->ri", row_table, row_totals, precision=lax.Precision.HIGHEST)
    from_rows = swap(row_part.reshape(n_mem, NB_DEV, side), "mem")
    cols_by_half = cols % NB_DEV * n_clu + cols // NB_DEV
    col_part = call_on_tiles(
        functools.partial(totals_kernel, 0), (cols_by_half, count), (), tiles,
        shape((col_blocks, side), F32), (col_space,), LIMIT,
    )

    kinds = seed_class.reshape(NB_DEV, side)
    weight = seed_weight.reshape(NB_DEV, side)
    known = jnp.concatenate([col_part.astype(BF16), split3(weight), kinds.astype(BF16)])
    classes_now = jnp.arange(CLASSES, dtype=jnp.int32)[:, None]
    labels = jnp.where(kinds[:, None] == classes_now, weight[:, None], jnp.float32(0.0))
    known, labels, from_rows = lax.optimization_barrier((known, labels, from_rows))
    sent = jnp.concatenate([known, split3(jnp.sum(from_rows, axis=0))])
    sent = jnp.pad(sent, ((0, -sent.shape[0] % 16), (0, 0)))
    got = swap(jnp.broadcast_to(sent[None], (n_clu,) + sent.shape), "clu")

    row_sum, col_root = call_on_tiles(
        first_kernel, (rows, count, cols_by_half), (got,), tiles,
        (shape((n_mem, height, side), BF16), shape((col_blocks, side), F32)),
        (row_space, col_space, (n_clu, got.shape[1] - col_blocks, side), (col_blocks, side)), LIMIT,
    )
    inverse_root = lax.dynamic_index_in_dim(
        col_root.reshape(NB_DEV, n_clu, side), lax.axis_index("clu"), 1, keepdims=False
    )
    own = jnp.concatenate([inverse_root * weight, kinds.astype(F32)], axis=1)
    peers = max(n_mem, n_clu)
    def panel_of(value, kind):
        kind = kind.reshape(-1, 1, side)
        panel = jnp.where(kind == classes_now.astype(BF16), value.reshape(-1, 1, side), jnp.zeros((), BF16))
        return panel.reshape(-1, height, side)

    scale = inverse_root[:, None]

    def forward(col_panel):
        return call_on_tiles(
            functools.partial(products_kernel, 1), (rows, count, cols), (col_panel,), tiles,
            shape((n_mem, height, side), BF16), (row_space, col_space), LIMIT,
        )

    def backward(row_panel, dtype):
        return call_on_tiles(
            functools.partial(products_kernel, 0), (cols, count, rows), (row_panel,), tiles,
            shape((n_clu, height, side), dtype), (col_space, row_space), LIMIT,
        )

    def total(parts):
        return jnp.sum(parts.astype(F32), axis=0)

    lanes = CLASSES * side

    def wide(partials, tail):
        partials = partials.reshape(-1, NB_DEV, lanes)
        tail = jnp.broadcast_to(tail[None].astype(BF16), partials.shape[:1] + tail.shape)
        return jnp.concatenate([partials, tail], axis=2)

    def narrow(image):
        return image[:, :lanes].reshape(NB_DEV, CLASSES, side)

    from_mem = swap(wide(row_sum, own), "mem")
    col_sum = backward(
        panel_of(from_mem[:, :, lanes : lanes + side], from_mem[:, :, lanes + side :]), F32
    )
    from_cols = swap(col_sum, "clu")
    row_image = narrow(total(from_mem)).reshape(height, side)
    first, sent = pl.pallas_call(
        middle_kernel,
        out_shape=(shape((height, side), F32), shape((peers, height, side), BF16)),
        compiler_params=pltpu.CompilerParams(vmem_limit_bytes=LIMIT << 20),
    )(from_cols, row_image, jnp.broadcast_to(scale, (NB_DEV, CLASSES, side)).reshape(height, side))
    first = first.reshape(NB_DEV, CLASSES, side)

    col_scaled = swap(sent[:n_clu], "clu")
    sent, col_scaled = lax.optimization_barrier((sent, col_scaled))
    row_scaled = swap(sent[:n_mem], "mem")
    def pieces_row(x):
        pieces = split3(x)
        return jnp.pad(pieces, (0, side - pieces.shape[0]))

    def whole(pieces, count):
        return jnp.sum(pieces[: 3 * count].reshape(3, count), axis=0)

    early = jnp.concatenate(
        [
            jnp.sum(labels * labels, axis=(0, 2)),
            jnp.sum(labels * first, axis=(0, 2)),
            jnp.sum(first * first, axis=(0, 2)),
        ]
    )
    row_sum = forward(col_scaled)
    row_wide = wide(row_sum, jnp.pad(pieces_row(early)[None], ((0, NB_DEV - 1), (0, 0))))
    row_sum, row_wide, row_scaled = lax.optimization_barrier((row_sum, row_wide, row_scaled))
    dots = 2.0 * jnp.sum(
        (row_sum.astype(F32) * row_scaled.astype(F32)).reshape(-1, NB_DEV, CLASSES, side), axis=(0, 1, 3)
    )
    is_late = jnp.arange(NB_DEV)[:, None] == 1
    spare = jnp.where(is_late, pieces_row(dots), row_wide[:, :, lanes:])
    from_rows = swap(lax.dynamic_update_slice(row_wide, spare, (0, 0, lanes)), "mem")
    col_sum = backward(row_scaled, BF16)
    col_sum, from_rows = lax.optimization_barrier((col_sum, from_rows))
    from_rows = lax.optimization_barrier(total(from_rows))
    line = from_rows[:, lanes:]
    line = pieces_row(jnp.concatenate([whole(line[0], 3 * CLASSES), whole(line[1], CLASSES)]))
    line = jnp.broadcast_to(jnp.pad(line[None], ((0, CLASSES - 1), (0, 0))), (n_clu, CLASSES, side))
    from_cols = swap(jnp.concatenate([col_sum, line], axis=1), "clu")
    from_cols, row_image = lax.optimization_barrier((from_cols, narrow(from_rows)))
    from_cols = total(from_cols)
    image = from_cols[:height].reshape(NB_DEV, CLASSES, side) + row_image
    second = scale * image
    m0, m1, m2, m3 = whole(from_cols[height], 4 * CLASSES).reshape(4, CLASSES)[:, :, None]

    ratio = m1 / m0
    qq = m2 - ratio * m1
    q_image = m3 - ratio * (2.0 * qq + ratio * m1)
    alpha0 = m0 / (m0 - DAMP * m1)
    pace = DAMP * alpha0
    beta = pace * pace * qq / m0
    alpha1 = qq / (qq - DAMP * q_image - DAMP * pace * qq * (qq / m0))
    q = first - ratio * labels
    q_applied = q - DAMP * (second - ratio * first)
    direction = pace * q + beta * labels
    applied = pace * q_applied + beta * (labels - DAMP * first)
    scores = alpha0 * labels + alpha1 * direction
    residual = pace * q - alpha1 * applied

    def out(x):
        return jnp.swapaxes(x, 0, 1).reshape(CLASSES, NB_DEV * side)

    return (out(scores), out(residual))


def solution(mesh):
    in_specs = (
        P(("clu", "mem")),
        P(("clu", "mem")),
        P("clu", "mem", None, None, None),
        P("clu", "mem", None),
        P("clu", "mem", None),
        P("clu", "mem"),
    )
    out_specs = (P(None, ("clu", "mem")), P(None, ("clu", "mem")))
    return jax.shard_map(
        on_device, mesh=mesh, in_specs=in_specs, out_specs=out_specs, check_vma=False
    )
```

```python
import functools

import jax
import jax.numpy as jnp
from jax import lax
from jax.experimental import pallas as pl
from jax.experimental.pallas import tpu as pltpu
from jax.sharding import PartitionSpec as P

CLASSES = 8
NB_DEV = 2
DAMP = 0.99
F32 = jnp.float32
BF16 = jnp.bfloat16
LIMIT = 8
KIND_AT = 3 * NB_DEV
SUMS_AT = KIND_AT + NB_DEV


def swap(parts, axis):
    return lax.all_to_all(parts, axis, 0, 0, tiled=True)


def split3(x):
    high = lax.reduce_precision(x, 8, 7)
    rest = x - high
    mid = lax.reduce_precision(rest, 8, 7)
    return jnp.concatenate([high, mid, rest - mid]).astype(BF16)


def sum_slots(into_ref, count_ref, tiles_ref, acc, left_of, side):
    acc[...] = jnp.zeros_like(acc)
    for slot in range(tiles_ref.shape[0]):
        used = jnp.where(slot < count_ref[0], 1.0, 0.0)
        product = lax.dot_general(
            left_of(slot), tiles_ref[slot], (((1,), (side,)), ((), ())), preferred_element_type=F32
        )
        acc[into_ref[slot]] += used * product


def totals_kernel(side, into_ref, count_ref, tiles_ref, out, acc):
    ones = jnp.ones((CLASSES, tiles_ref.shape[2]), BF16)
    sum_slots(into_ref, count_ref, tiles_ref, acc, lambda slot: ones, side)
    out[...] = acc[:, 0, :]


def products_kernel(side, into_ref, count_ref, from_ref, panel, tiles_ref, out, acc, wide):
    wide[...] = panel[...].astype(F32).reshape(wide.shape)
    sum_slots(
        into_ref, count_ref, tiles_ref, acc, lambda slot: wide[from_ref[slot]].astype(BF16), side
    )
    out[...] = acc[...].reshape(out.shape).astype(out.dtype)


def first_kernel(into_ref, count_ref, from_ref, got, tiles_ref, out, root, acc, wide, known, value):
    n_clu = got.shape[0]
    blocks = NB_DEV * n_clu
    known[...] = got[:, blocks:].astype(F32)
    totals = jnp.sum(got[:, :blocks].astype(F32), axis=0)

    def whole(row):
        return known[:, row, :] + known[:, row + NB_DEV, :] + known[:, row + 2 * NB_DEV, :]

    for b in range(NB_DEV):
        part = slice(b * n_clu, (b + 1) * n_clu)
        root[part] = lax.rsqrt(1.0 + totals[part] + whole(SUMS_AT + b))
        value[part] = root[part] * whole(b)
    for b in range(NB_DEV):
        for peer in range(n_clu):
            block = b * n_clu + peer
            row = (CLASSES, value.shape[1])
            kind = jnp.broadcast_to(known[peer, KIND_AT + b : KIND_AT + b + 1, :], row)
            here = jnp.broadcast_to(value[block : block + 1, :], row)
            classes_now = lax.broadcasted_iota(jnp.int32, row, 0).astype(F32)
            wide[block] = jnp.where(kind == classes_now, here, 0.0)
    sum_slots(
        into_ref, count_ref, tiles_ref, acc, lambda slot: wide[from_ref[slot]].astype(BF16), 1
    )
    out[...] = acc[...].reshape(out.shape).astype(out.dtype)


def middle_kernel(from_cols, row_image, scale, first, sent):
    scale = scale[...]
    image = scale * (jnp.sum(from_cols[...], axis=0) + row_image[...])
    first[...] = image
    sent[...] = jnp.broadcast_to((scale * image).astype(BF16)[None], sent.shape)


def call_on_tiles(kernel, index, panels, tiles, out, scratch, limit):
    slots, side = tiles.shape[0], tiles.shape[1]

    smem, vmem = pl.BlockSpec(memory_space=pltpu.SMEM), pl.BlockSpec(memory_space=pltpu.VMEM)
    return pl.pallas_call(
        kernel,
        in_specs=[smem] * len(index) + [vmem] * (len(panels) + 1),
        out_specs=jax.tree.map(lambda _: vmem, out),
        scratch_shapes=[pltpu.VMEM(x, F32) for x in scratch],
        out_shape=out,
        compiler_params=pltpu.CompilerParams(vmem_limit_bytes=limit << 20),
        cost_estimate=pl.CostEstimate(
            flops=2 * CLASSES * slots * side * side,
            bytes_accessed=2 * slots * side * side,
            transcendentals=0,
        ),
    )(*index, *panels, tiles)


def on_device(seed_class, seed_weight, tile_values, tile_rows, tile_cols, tile_count):
    tiles = tile_values[0, 0]
    rows = tile_rows[0, 0]
    cols = tile_cols[0, 0]
    count = tile_count[0]
    slots, side = tiles.shape[0], tiles.shape[1]
    n_mem, n_clu = lax.axis_size("mem"), lax.axis_size("clu")
    row_blocks, col_blocks = NB_DEV * n_mem, NB_DEV * n_clu
    height = NB_DEV * CLASSES
    row_space, col_space = (row_blocks, CLASSES, side), (col_blocks, CLASSES, side)
    shape = jax.ShapeDtypeStruct

    used = jnp.arange(slots, dtype=jnp.int32) < count
    blocks = jnp.arange(row_blocks, dtype=jnp.int32)[:, None]
    row_table = ((rows[None, :] == blocks) & used).astype(F32)
    row_totals = jnp.sum(tiles, axis=2, dtype=F32)
    row_part = jnp.einsum("rt,ti->ri", row_table, row_totals, precision=lax.Precision.HIGHEST)
    from_rows = swap(row_part.reshape(n_mem, NB_DEV, side), "mem")
    cols_by_half = cols % NB_DEV * n_clu + cols // NB_DEV
    col_part = call_on_tiles(
        functools.partial(totals_kernel, 0), (cols_by_half, count), (), tiles,
        shape((col_blocks, side), F32), (col_space,), LIMIT,
    )

    kinds = seed_class.reshape(NB_DEV, side)
    weight = seed_weight.reshape(NB_DEV, side)
    known = jnp.concatenate([col_part.astype(BF16), split3(weight), kinds.astype(BF16)])
    classes_now = jnp.arange(CLASSES, dtype=jnp.int32)[:, None]
    labels = jnp.where(kinds[:, None] == classes_now, weight[:, None], jnp.float32(0.0))
    table = jnp.broadcast_to(classes_now.astype(BF16), (CLASSES, side))
    known, labels, table, from_rows = lax.optimization_barrier((known, labels, table, from_rows))
    sent = jnp.concatenate([known, split3(jnp.sum(from_rows, axis=0))])
    sent = jnp.pad(sent, ((0, -sent.shape[0] % 16), (0, 0)))
    got = swap(jnp.broadcast_to(sent[None], (n_clu,) + sent.shape), "clu")

    row_sum, col_root = call_on_tiles(
        first_kernel, (rows, count, cols_by_half), (got,), tiles,
        (shape((n_mem, height, side), BF16), shape((col_blocks, side), F32)),
        (row_space, col_space, (n_clu, got.shape[1] - col_blocks, side), (col_blocks, side)), LIMIT,
    )
    inverse_root = lax.dynamic_index_in_dim(
        col_root.reshape(NB_DEV, n_clu, side), lax.axis_index("clu"), 1, keepdims=False
    )
    own = jnp.concatenate([inverse_root * weight, kinds.astype(F32)], axis=1)
    peers = max(n_mem, n_clu)
    def panel_of(value, kind):
        kind = kind.reshape(-1, 1, side)
        panel = jnp.where(kind == table, value.reshape(-1, 1, side), jnp.zeros((), BF16))
        return panel.reshape(-1, height, side)

    scale = inverse_root[:, None]

    def forward(col_panel):
        return call_on_tiles(
            functools.partial(products_kernel, 1), (rows, count, cols), (col_panel,), tiles,
            shape((n_mem, height, side), BF16), (row_space, col_space), LIMIT,
        )

    def backward(row_panel, dtype):
        return call_on_tiles(
            functools.partial(products_kernel, 0), (cols, count, rows), (row_panel,), tiles,
            shape((n_clu, height, side), dtype), (col_space, row_space), LIMIT,
        )

    def total(parts):
        return jnp.sum(parts.astype(F32), axis=0)

    lanes = CLASSES * side

    def wide(partials, tail):
        partials = partials.reshape(-1, NB_DEV, lanes)
        tail = jnp.broadcast_to(tail[None].astype(BF16), partials.shape[:1] + tail.shape)
        return jnp.concatenate([partials, tail], axis=2)

    def narrow(image):
        return image[:, :lanes].reshape(NB_DEV, CLASSES, side)

    from_mem = swap(wide(row_sum, own), "mem")
    col_sum = backward(
        panel_of(from_mem[:, :, lanes : lanes + side], from_mem[:, :, lanes + side :]), F32
    )
    from_cols = swap(col_sum, "clu")
    row_image = narrow(total(from_mem)).reshape(height, side)
    first, sent = pl.pallas_call(
        middle_kernel,
        out_shape=(shape((height, side), F32), shape((peers, height, side), BF16)),
        compiler_params=pltpu.CompilerParams(vmem_limit_bytes=LIMIT << 20),
    )(from_cols, row_image, jnp.broadcast_to(scale, (NB_DEV, CLASSES, side)).reshape(height, side))
    first = first.reshape(NB_DEV, CLASSES, side)

    col_scaled = swap(sent[:n_clu], "clu")
    sent, col_scaled = lax.optimization_barrier((sent, col_scaled))
    row_scaled = swap(sent[:n_mem], "mem")
    def pieces_row(x):
        pieces = split3(x)
        return jnp.pad(pieces, (0, side - pieces.shape[0]))

    def whole(pieces, count):
        return jnp.sum(pieces[: 3 * count].reshape(3, count), axis=0)

    early = jnp.concatenate(
        [
            jnp.sum(labels * labels, axis=(0, 2)),
            jnp.sum(labels * first, axis=(0, 2)),
            jnp.sum(first * first, axis=(0, 2)),
        ]
    )
    row_sum = forward(col_scaled)
    row_wide = wide(row_sum, jnp.pad(pieces_row(early)[None], ((0, NB_DEV - 1), (0, 0))))
    row_sum, row_wide, row_scaled = lax.optimization_barrier((row_sum, row_wide, row_scaled))
    dots = 2.0 * jnp.sum(
        (row_sum.astype(F32) * row_scaled.astype(F32)).reshape(-1, NB_DEV, CLASSES, side), axis=(0, 1, 3)
    )
    is_late = jnp.arange(NB_DEV)[:, None] == 1
    spare = jnp.where(is_late, pieces_row(dots), row_wide[:, :, lanes:])
    from_rows = swap(lax.dynamic_update_slice(row_wide, spare, (0, 0, lanes)), "mem")
    col_sum = backward(row_scaled, BF16)
    col_sum, from_rows = lax.optimization_barrier((col_sum, from_rows))
    from_rows = lax.optimization_barrier(total(from_rows))
    line = from_rows[:, lanes:]
    line = pieces_row(jnp.concatenate([whole(line[0], 3 * CLASSES), whole(line[1], CLASSES)]))
    line = jnp.broadcast_to(jnp.pad(line[None], ((0, CLASSES - 1), (0, 0))), (n_clu, CLASSES, side))
    from_cols = swap(jnp.concatenate([col_sum, line], axis=1), "clu")
    from_cols, row_image = lax.optimization_barrier((from_cols, narrow(from_rows)))
    from_cols = total(from_cols)
    image = from_cols[:height].reshape(NB_DEV, CLASSES, side) + row_image
    second = scale * image
    m0, m1, m2, m3 = whole(from_cols[height], 4 * CLASSES).reshape(4, CLASSES)[:, :, None]

    ratio = m1 / m0
    qq = m2 - ratio * m1
    q_image = m3 - ratio * (2.0 * qq + ratio * m1)
    alpha0 = m0 / (m0 - DAMP * m1)
    pace = DAMP * alpha0
    beta = pace * pace * qq / m0
    alpha1 = qq / (qq - DAMP * q_image - DAMP * pace * qq * (qq / m0))
    q = first - ratio * labels
    q_applied = q - DAMP * (second - ratio * first)
    direction = pace * q + beta * labels
    applied = pace * q_applied + beta * (labels - DAMP * first)
    scores = alpha0 * labels + alpha1 * direction
    residual = pace * q - alpha1 * applied

    def out(x):
        return jnp.swapaxes(x, 0, 1).reshape(CLASSES, NB_DEV * side)

    return (out(scores), out(residual))


def solution(mesh):
    in_specs = (
        P(("clu", "mem")),
        P(("clu", "mem")),
        P("clu", "mem", None, None, None),
        P("clu", "mem", None),
        P("clu", "mem", None),
        P("clu", "mem"),
    )
    out_specs = (P(None, ("clu", "mem")), P(None, ("clu", "mem")))
    return jax.shard_map(
        on_device, mesh=mesh, in_specs=in_specs, out_specs=out_specs, check_vma=False
    )
```

```python
import functools

import jax
import jax.numpy as jnp
from jax import lax
from jax.experimental import pallas as pl
from jax.experimental.pallas import tpu as pltpu
from jax.sharding import PartitionSpec as P

CLASSES = 8
NB_DEV = 2
DAMP = 0.99
F32 = jnp.float32
BF16 = jnp.bfloat16
LIMIT = 8
KIND_AT = 3 * NB_DEV
SUMS_AT = KIND_AT + NB_DEV


def swap(parts, axis):
    return lax.all_to_all(parts, axis, 0, 0, tiled=True)


def split3(x):
    high = lax.reduce_precision(x, 8, 7)
    rest = x - high
    mid = lax.reduce_precision(rest, 8, 7)
    return jnp.concatenate([high, mid, rest - mid]).astype(BF16)


def sum_slots(into_ref, count_ref, tiles_ref, acc, left_of, side):
    acc[...] = jnp.zeros_like(acc)
    for slot in range(tiles_ref.shape[0]):
        used = jnp.where(slot < count_ref[0], 1.0, 0.0)
        product = lax.dot_general(
            left_of(slot), tiles_ref[slot], (((1,), (side,)), ((), ())), preferred_element_type=F32
        )
        acc[into_ref[slot]] += used * product


def totals_kernel(side, into_ref, count_ref, tiles_ref, out, acc):
    ones = jnp.ones((CLASSES, tiles_ref.shape[2]), BF16)
    sum_slots(into_ref, count_ref, tiles_ref, acc, lambda slot: ones, side)
    out[...] = acc[:, 0, :]


def products_kernel(side, into_ref, count_ref, from_ref, panel, tiles_ref, out, acc, wide):
    wide[...] = panel[...].astype(F32).reshape(wide.shape)
    sum_slots(
        into_ref, count_ref, tiles_ref, acc, lambda slot: wide[from_ref[slot]].astype(BF16), side
    )
    out[...] = acc[...].reshape(out.shape).astype(out.dtype)


def first_kernel(into_ref, count_ref, from_ref, got, tiles_ref, out, root, acc, wide, known, value):
    n_clu = got.shape[0]
    blocks = NB_DEV * n_clu
    known[...] = got[:, blocks:].astype(F32)
    totals = jnp.sum(got[:, :blocks].astype(F32), axis=0)

    def whole(row):
        return known[:, row, :] + known[:, row + NB_DEV, :] + known[:, row + 2 * NB_DEV, :]

    for b in range(NB_DEV):
        part = slice(b * n_clu, (b + 1) * n_clu)
        root[part] = lax.rsqrt(1.0 + totals[part] + whole(SUMS_AT + b))
        value[part] = root[part] * whole(b)
    for b in range(NB_DEV):
        for peer in range(n_clu):
            block = b * n_clu + peer
            row = (CLASSES, value.shape[1])
            kind = jnp.broadcast_to(known[peer, KIND_AT + b : KIND_AT + b + 1, :], row)
            here = jnp.broadcast_to(value[block : block + 1, :], row)
            classes_now = lax.broadcasted_iota(jnp.int32, row, 0).astype(F32)
            wide[block] = jnp.where(kind == classes_now, here, 0.0)
    sum_slots(
        into_ref, count_ref, tiles_ref, acc, lambda slot: wide[from_ref[slot]].astype(BF16), 1
    )
    out[...] = acc[...].reshape(out.shape).astype(out.dtype)


def middle_kernel(from_cols, row_image, scale, first, sent):
    scale = scale[...]
    image = scale * (jnp.sum(from_cols[...], axis=0) + row_image[...])
    first[...] = image
    sent[...] = jnp.broadcast_to((scale * image).astype(BF16)[None], sent.shape)


def call_on_tiles(kernel, index, panels, tiles, out, scratch, limit):
    slots, side = tiles.shape[0], tiles.shape[1]

    smem, vmem = pl.BlockSpec(memory_space=pltpu.SMEM), pl.BlockSpec(memory_space=pltpu.VMEM)
    return pl.pallas_call(
        kernel,
        in_specs=[smem] * len(index) + [vmem] * (len(panels) + 1),
        out_specs=jax.tree.map(lambda _: vmem, out),
        scratch_shapes=[pltpu.VMEM(x, F32) for x in scratch],
        out_shape=out,
        compiler_params=pltpu.CompilerParams(vmem_limit_bytes=limit << 20),
        cost_estimate=pl.CostEstimate(
            flops=2 * CLASSES * slots * side * side,
            bytes_accessed=2 * slots * side * side,
            transcendentals=0,
        ),
    )(*index, *panels, tiles)


def on_device(seed_class, seed_weight, tile_values, tile_rows, tile_cols, tile_count):
    tiles = tile_values[0, 0]
    rows = tile_rows[0, 0]
    cols = tile_cols[0, 0]
    count = tile_count[0]
    slots, side = tiles.shape[0], tiles.shape[1]
    n_mem, n_clu = lax.axis_size("mem"), lax.axis_size("clu")
    row_blocks, col_blocks = NB_DEV * n_mem, NB_DEV * n_clu
    height = NB_DEV * CLASSES
    row_space, col_space = (row_blocks, CLASSES, side), (col_blocks, CLASSES, side)
    shape = jax.ShapeDtypeStruct

    used = jnp.arange(slots, dtype=jnp.int32) < count
    blocks = jnp.arange(row_blocks, dtype=jnp.int32)[:, None]
    row_table = ((rows[None, :] == blocks) & used).astype(F32)
    row_totals = jnp.sum(tiles, axis=2, dtype=F32)
    row_part = jnp.einsum("rt,ti->ri", row_table, row_totals, precision=lax.Precision.HIGHEST)
    from_rows = swap(row_part.reshape(n_mem, NB_DEV, side), "mem")
    cols_by_half = cols % NB_DEV * n_clu + cols // NB_DEV
    col_part = call_on_tiles(
        functools.partial(totals_kernel, 0), (cols_by_half, count), (), tiles,
        shape((col_blocks, side), F32), (col_space,), LIMIT,
    )

    kinds = seed_class.reshape(NB_DEV, side)
    weight = seed_weight.reshape(NB_DEV, side)
    known = jnp.concatenate([col_part.astype(BF16), split3(weight), kinds.astype(BF16)])
    classes_now = jnp.arange(CLASSES, dtype=jnp.int32)[:, None]
    labels = jnp.where(kinds[:, None] == classes_now, weight[:, None], jnp.float32(0.0))
    table = jnp.broadcast_to(classes_now.astype(BF16), (CLASSES, side))
    place = lax.axis_index("clu").astype(jnp.uint32)
    known, labels, table, place, from_rows = lax.optimization_barrier((known, labels, table, place, from_rows))
    sent = jnp.concatenate([known, split3(jnp.sum(from_rows, axis=0))])
    sent = jnp.pad(sent, ((0, -sent.shape[0] % 16), (0, 0)))
    got = swap(jnp.broadcast_to(sent[None], (n_clu,) + sent.shape), "clu")

    row_sum, col_root = call_on_tiles(
        first_kernel, (rows, count, cols_by_half), (got,), tiles,
        (shape((n_mem, height, side), BF16), shape((col_blocks, side), F32)),
        (row_space, col_space, (n_clu, got.shape[1] - col_blocks, side), (col_blocks, side)), LIMIT,
    )
    none = jnp.zeros((), jnp.uint32)
    inverse_root = lax.dynamic_slice(
        col_root.reshape(NB_DEV, n_clu, side), (none, place, none), (NB_DEV, 1, side)
    ).reshape(NB_DEV, side)
    own = jnp.concatenate([inverse_root * weight, kinds.astype(F32)], axis=1)
    peers = max(n_mem, n_clu)
    def panel_of(value, kind):
        kind = kind.reshape(-1, 1, side)
        panel = jnp.where(kind == table, value.reshape(-1, 1, side), jnp.zeros((), BF16))
        return panel.reshape(-1, height, side)

    scale = inverse_root[:, None]

    def forward(col_panel):
        return call_on_tiles(
            functools.partial(products_kernel, 1), (rows, count, cols), (col_panel,), tiles,
            shape((n_mem, height, side), BF16), (row_space, col_space), LIMIT,
        )

    def backward(row_panel, dtype):
        return call_on_tiles(
            functools.partial(products_kernel, 0), (cols, count, rows), (row_panel,), tiles,
            shape((n_clu, height, side), dtype), (col_space, row_space), LIMIT,
        )

    def total(parts):
        return jnp.sum(parts.astype(F32), axis=0)

    lanes = CLASSES * side

    def wide(partials, tail):
        partials = partials.reshape(-1, NB_DEV, lanes)
        tail = jnp.broadcast_to(tail[None].astype(BF16), partials.shape[:1] + tail.shape)
        return jnp.concatenate([partials, tail], axis=2)

    def narrow(image):
        return image[:, :lanes].reshape(NB_DEV, CLASSES, side)

    from_mem = swap(wide(row_sum, own), "mem")
    col_sum = backward(
        panel_of(from_mem[:, :, lanes : lanes + side], from_mem[:, :, lanes + side :]), F32
    )
    from_cols = swap(col_sum, "clu")
    row_image = narrow(total(from_mem)).reshape(height, side)
    first, sent = pl.pallas_call(
        middle_kernel,
        out_shape=(shape((height, side), F32), shape((peers, height, side), BF16)),
        compiler_params=pltpu.CompilerParams(vmem_limit_bytes=LIMIT << 20),
    )(from_cols, row_image, jnp.broadcast_to(scale, (NB_DEV, CLASSES, side)).reshape(height, side))
    first = first.reshape(NB_DEV, CLASSES, side)

    col_scaled = swap(sent[:n_clu], "clu")
    sent, col_scaled = lax.optimization_barrier((sent, col_scaled))
    row_scaled = swap(sent[:n_mem], "mem")
    def pieces_row(x):
        pieces = split3(x)
        return jnp.pad(pieces, (0, side - pieces.shape[0]))

    def whole(pieces, count):
        return jnp.sum(pieces[: 3 * count].reshape(3, count), axis=0)

    early = jnp.concatenate(
        [
            jnp.sum(labels * labels, axis=(0, 2)),
            jnp.sum(labels * first, axis=(0, 2)),
            jnp.sum(first * first, axis=(0, 2)),
        ]
    )
    row_sum = forward(col_scaled)
    row_wide = wide(row_sum, jnp.pad(pieces_row(early)[None], ((0, NB_DEV - 1), (0, 0))))
    row_sum, row_wide, row_scaled = lax.optimization_barrier((row_sum, row_wide, row_scaled))
    dots = 2.0 * jnp.sum(
        (row_sum.astype(F32) * row_scaled.astype(F32)).reshape(-1, NB_DEV, CLASSES, side), axis=(0, 1, 3)
    )
    is_late = jnp.arange(NB_DEV)[:, None] == 1
    spare = jnp.where(is_late, pieces_row(dots), row_wide[:, :, lanes:])
    from_rows = swap(lax.dynamic_update_slice(row_wide, spare, (0, 0, lanes)), "mem")
    col_sum = backward(row_scaled, BF16)
    col_sum, from_rows = lax.optimization_barrier((col_sum, from_rows))
    from_rows = lax.optimization_barrier(total(from_rows))
    line = from_rows[:, lanes:]
    line = pieces_row(jnp.concatenate([whole(line[0], 3 * CLASSES), whole(line[1], CLASSES)]))
    line = jnp.broadcast_to(jnp.pad(line[None], ((0, CLASSES - 1), (0, 0))), (n_clu, CLASSES, side))
    from_cols = swap(jnp.concatenate([col_sum, line], axis=1), "clu")
    from_cols, row_image = lax.optimization_barrier((from_cols, narrow(from_rows)))
    from_cols = total(from_cols)
    image = from_cols[:height].reshape(NB_DEV, CLASSES, side) + row_image
    second = scale * image
    m0, m1, m2, m3 = whole(from_cols[height], 4 * CLASSES).reshape(4, CLASSES)[:, :, None]

    ratio = m1 / m0
    qq = m2 - ratio * m1
    q_image = m3 - ratio * (2.0 * qq + ratio * m1)
    alpha0 = m0 / (m0 - DAMP * m1)
    pace = DAMP * alpha0
    beta = pace * pace * qq / m0
    alpha1 = qq / (qq - DAMP * q_image - DAMP * pace * qq * (qq / m0))
    q = first - ratio * labels
    q_applied = q - DAMP * (second - ratio * first)
    direction = pace * q + beta * labels
    applied = pace * q_applied + beta * (labels - DAMP * first)
    scores = alpha0 * labels + alpha1 * direction
    residual = pace * q - alpha1 * applied

    def out(x):
        return jnp.swapaxes(x, 0, 1).reshape(CLASSES, NB_DEV * side)

    return (out(scores), out(residual))


def solution(mesh):
    in_specs = (
        P(("clu", "mem")),
        P(("clu", "mem")),
        P("clu", "mem", None, None, None),
        P("clu", "mem", None),
        P("clu", "mem", None),
        P("clu", "mem"),
    )
    out_specs = (P(None, ("clu", "mem")), P(None, ("clu", "mem")))
    return jax.shard_map(
        on_device, mesh=mesh, in_specs=in_specs, out_specs=out_specs, check_vma=False
    )
```
